32 devices in a mesh: ctx: 8 (over y, x, core), fsdp: 4 (over z).
Axes of the slice: x: 2, y: 2, z: 4, core: 2. Of those that a mesh axis runs over, the one named last changes fastest.
Arguments:
- states: bfloat16 [4, 3072, 1024], P('fsdp', 'ctx'), may hold values from -6 to 6
- norm_gain: float32 [512], replicated, may hold values from 0.1 to 1.9
- in_proj: bfloat16 [1024, 512], P('fsdp'), may hold values from -0.25 to 0.25
- conv_taps: float32 [2, 7, 1024], replicated, may hold values from -2 to 2
- dilations: int32 [2], replicated, may hold values from 1 to 64, as said below
- out_proj: bfloat16 [1024, 512], P('fsdp'), may hold values from -0.1875 to 0.1875
- cotangent: bfloat16 [4, 3072, 1024], P('fsdp', 'ctx'), may hold values from -0.0390625 to 0.0390625
Outputs:
- block_out: bfloat16 [4, 3072, 1024], P('fsdp', 'ctx')
- grad_in_proj: float32 [1024, 512], P('fsdp')
- grad_out_proj: float32 [1024, 512], P('fsdp')
- grad_taps: float32 [2, 7, 1024], replicated
The draws below stay inside these ranges and needn't reach their ends.
Inputs may be any that keep to these rules, and one draw needn't show every extreme that they name: `dilations`: each dilation is a power of two; exactly one equals 64, the other is smaller.
All inputs are finite; a program needn't handle non-finite values.
Results may differ from the reference program's by a relative error of at most 0.0095.
Values may be sent and summed in bfloat16 or wider, within the bound.
A program may use at most 128 MiB of HBM per device.

```python
import math
import jax
import jax.numpy as jnp
from jax import lax

D = 1024
H = 512
INNER = 1024
KERNEL = 7
NCONV = 2
MAXDIL = 64
SEQS = 4
LENGTH = 3072


def draw_dilations(key, part):
    key = jax.random.fold_in(key, 7)
    top_power = int(math.log2(MAXDIL))
    lower_power = jax.random.randint(jax.random.fold_in(key, 11), (), 0, top_power)
    chosen = jax.random.randint(jax.random.fold_in(key, 12), (), 0, NCONV)
    powers = jnp.where(jnp.arange(NCONV) == chosen, top_power, lower_power).astype(jnp.int32)
    return jnp.left_shift(jnp.ones((NCONV,), jnp.int32), powers)


def steps_of(key, extent, pieces, low, top_value):
    def one(position, shards_of):
        draws = jax.random.uniform(jax.random.fold_in(jax.random.fold_in(key, 6), position), (shards_of,), jnp.float32, low / len(pieces), top_value / len(pieces))
        return jnp.repeat(jnp.exp(draws), extent[position] // shards_of).reshape((-1,) + (1,) * (len(extent) - position - 1))

    loudness = one(*pieces[0])
    for cut in pieces[1:]:
        loudness = loudness * one(*cut)
    return loudness


def noise(rng, extent, width, bound, shards=(), kind=jnp.bfloat16):
    entries = width * jax.random.normal(rng, extent, jnp.float32)
    if shards:
        entries = entries * steps_of(rng, extent, shards, -0.22, 0.18)
    return jnp.clip(entries, -bound, bound).astype(kind)


def setup_inputs(seed: int = 0) -> dict:
    arg_keys = jax.random.split(jax.random.key(seed), 8)
    return {
        "states": noise(arg_keys[0], (SEQS, LENGTH, D), 1.0, 6.0, ((0, 4), (1, 8))),
        "norm_gain": jnp.clip(1.0 + 0.18 * jax.random.normal(arg_keys[1], (H,), jnp.float32), 0.1, 1.9),
        "in_proj": noise(arg_keys[2], (INNER, H), H ** -0.5, 0.25, ((0, 4),)),
        "conv_taps": noise(arg_keys[3], (NCONV, KERNEL, INNER), KERNEL ** -0.5, 2.0, (), jnp.float32),
        "dilations": draw_dilations(jax.random.fold_in(arg_keys[7], 71), 0),
        "out_proj": noise(arg_keys[5], (INNER, H), INNER ** -0.5, 0.1875, ((0, 4),)),
        "cotangent": noise(arg_keys[6], (SEQS, LENGTH, D), (2 * LENGTH * SEQS) ** -0.5, 0.0390625, ((0, 4), (1, 8))),
    }


norm_eps = 1e-05

def normalize(strand, norm_gain):
    floats = strand.astype(jnp.float32)
    inverse = lax.rsqrt(lax.optimization_barrier(jnp.mean(floats * floats, axis=-1, keepdims=True)) + norm_eps)
    return (floats * inverse * norm_gain).astype(jnp.bfloat16)

def tap_start(dilation, tap_index, tap_count, looks_ahead, margin):
    stride_rows = dilation * (tap_count - 1 - tap_index)
    if looks_ahead:
        return stride_rows
    return margin - stride_rows

def apply_taps(extended, tap_weights, dilation, tok_rows, looks_ahead, margin):
    tap_count = tap_weights.shape[0]
    running = jnp.zeros((tok_rows, extended.shape[1]), jnp.float32)
    for tap_index in range(tap_count):
        window = lax.dynamic_slice_in_dim(extended, tap_start(dilation, tap_index, tap_count, looks_ahead, margin), tok_rows, 0)
        running = running + tap_weights[tap_index] * window.astype(jnp.float32)
    return running

def taps_gradient(upstream, extended, dilation, tap_count, looks_ahead, margin):
    tok_rows = upstream.shape[0]
    upstream_f = upstream.astype(jnp.float32)
    per_tap = []
    for tap_index in range(tap_count):
        window = lax.dynamic_slice_in_dim(extended, tap_start(dilation, tap_index, tap_count, looks_ahead, margin), tok_rows, 0)
        per_tap.append(lax.optimization_barrier(jnp.sum(upstream_f * window.astype(jnp.float32), axis=0)))
    return jnp.stack(per_tap)

def strand_pass(strand, upstream, norm_gain, in_proj, conv_taps, dilations, out_proj, margin):
    tok_rows = strand.shape[0]
    tap_count = conv_taps.shape[1]
    normed = normalize(strand, norm_gain)
    expanded = jnp.dot(normed, in_proj.T, preferred_element_type=jnp.float32).astype(jnp.bfloat16)
    zero_rim = jnp.zeros((margin, expanded.shape[1]), jnp.bfloat16)
    first_ext = jnp.concatenate([zero_rim, expanded], axis=0)
    first_conv = apply_taps(first_ext, conv_taps[0], dilations[0], tok_rows, False, margin).astype(jnp.bfloat16)
    second_ext = jnp.concatenate([zero_rim, first_conv], axis=0)
    second_conv = apply_taps(second_ext, conv_taps[1], dilations[1], tok_rows, False, margin)
    gate_sig = jax.nn.sigmoid(second_conv)
    activated = second_conv * gate_sig
    expanded_f = expanded.astype(jnp.float32)
    gated_hidden = (activated * expanded_f).astype(jnp.bfloat16)
    strand_out = (strand.astype(jnp.float32) + jnp.dot(gated_hidden, out_proj, preferred_element_type=jnp.float32)).astype(jnp.bfloat16)
    grad_out = jnp.dot(gated_hidden.T, upstream, preferred_element_type=jnp.float32)
    hidden_grad = jnp.dot(upstream, out_proj.T, preferred_element_type=jnp.float32)
    second_grad = (hidden_grad * expanded_f * gate_sig * (1.0 + second_conv * (1.0 - gate_sig))).astype(jnp.bfloat16)
    grad_ext = jnp.concatenate([second_grad, zero_rim], axis=0)
    first_grad = apply_taps(grad_ext, conv_taps[1], dilations[1], tok_rows, True, margin).astype(jnp.bfloat16)
    inner_ext = jnp.concatenate([first_grad, zero_rim], axis=0)
    expanded_grad = (hidden_grad * activated + apply_taps(inner_ext, conv_taps[0], dilations[0], tok_rows, True, margin)).astype(jnp.bfloat16)
    grad_in = jnp.dot(expanded_grad.T, normed, preferred_element_type=jnp.float32)
    grad_taps = jnp.stack([taps_gradient(first_grad, first_ext, dilations[0], tap_count, False, margin), taps_gradient(second_grad, second_ext, dilations[1], tap_count, False, margin)])
    return (strand_out, grad_in, grad_out, grad_taps)

def reference(states, norm_gain, in_proj, conv_taps, dilations, out_proj, cotangent):
    margin = (KERNEL - 1) * MAXDIL
    half_width = states.shape[2] // 2

    def one_sequence(totals, sequence_pair):
        seq_states, seq_grads = sequence_pair
        plain_pass = strand_pass(seq_states[:, :half_width], seq_grads[:, :half_width], norm_gain, in_proj, conv_taps, dilations, out_proj, margin)
        other_pass = strand_pass(seq_states[:, half_width:][::-1, ::-1], seq_grads[:, half_width:][::-1, ::-1], norm_gain, in_proj, conv_taps, dilations, out_proj, margin)
        joined = jnp.concatenate([plain_pass[0], other_pass[0][::-1, ::-1]], axis=1)
        totals = (totals[0] + plain_pass[1] + other_pass[1], totals[1] + plain_pass[2] + other_pass[2], totals[2] + plain_pass[3] + other_pass[3])
        return (totals, joined)
    zero_sums = (jnp.zeros(in_proj.shape, jnp.float32), jnp.zeros(out_proj.shape, jnp.float32), jnp.zeros(conv_taps.shape, jnp.float32))
    totals, blocks = lax.scan(one_sequence, zero_sums, (states, cotangent))
    return (blocks, totals[0], totals[1], totals[2])
```

```python
import jax
import jax.numpy as jnp
from jax import lax
from jax.sharding import PartitionSpec as P

KERNEL = 7
MAXDIL = 64


norm_eps = 1e-05


def passed_along(value, axis, by):
    length = lax.axis_size(axis)
    pairs = [(i, i + by) for i in range(length) if 0 <= i + by < length]
    return lax.ppermute(value, axis, pairs)


def normalize(strand, norm_gain):
    floats = strand.astype(jnp.float32)
    inverse = lax.rsqrt(jnp.mean(floats * floats, axis=-1, keepdims=True) + norm_eps)
    return (floats * inverse * norm_gain).astype(jnp.bfloat16)


def tap_start(dilation, tap_index, tap_count, looks_ahead, margin):
    stride_rows = dilation * (tap_count - 1 - tap_index)
    if looks_ahead:
        return stride_rows
    return margin - stride_rows


def apply_taps(extended, tap_weights, dilation, tok_rows, looks_ahead, margin):
    tap_count = tap_weights.shape[0]
    running = jnp.zeros((tok_rows, extended.shape[1]), jnp.float32)
    for tap_index in range(tap_count):
        window = lax.dynamic_slice_in_dim(
            extended, tap_start(dilation, tap_index, tap_count, looks_ahead, margin), tok_rows, 0
        )
        running = running + tap_weights[tap_index] * window.astype(jnp.float32)
    return running


def taps_gradient(upstream, extended, dilation, tap_count, looks_ahead, margin):
    tok_rows = upstream.shape[0]
    upstream_f = upstream.astype(jnp.float32)
    per_tap = []
    for tap_index in range(tap_count):
        window = lax.dynamic_slice_in_dim(
            extended, tap_start(dilation, tap_index, tap_count, looks_ahead, margin), tok_rows, 0
        )
        per_tap.append(jnp.sum(upstream_f * window.astype(jnp.float32), axis=0))
    return jnp.stack(per_tap)


def extend(values, backward):
    margin = (KERNEL - 1) * MAXDIL
    joined = []
    for strand in range(2):
        ahead = (strand == 1) != backward
        value = values[strand]
        if ahead:
            rim = passed_along(value[:margin], "ctx", -1)
            joined.append(jnp.concatenate([value, rim], axis=0))
        else:
            rim = passed_along(value[-margin:], "ctx", 1)
            joined.append(jnp.concatenate([rim, value], axis=0))
    return joined


def body(states, norm_gain, in_proj, conv_taps, dilations, out_proj, cotangent):
    margin = (KERNEL - 1) * MAXDIL
    half = states.shape[2] // 2
    rows = states.shape[1]
    taps = conv_taps.shape[1]
    own = in_proj.shape[0]
    both_proj = lax.all_gather(jnp.concatenate([in_proj, out_proj], axis=1), "fsdp", axis=0, tiled=True)
    full_in, full_out = both_proj[:, :half], both_proj[:, half:]
    w_in = [full_in, full_in[:, ::-1]]
    w_out = [full_out, full_out[:, ::-1]]
    gain = [norm_gain, norm_gain[::-1]]
    strands = [states[0, :, :half], states[0, :, half:]]
    ups = [cotangent[0, :, :half], cotangent[0, :, half:]]
    both = range(2)
    normed = [normalize(strands[s], gain[s]) for s in both]

    def mm(a, b, dims):
        return lax.dot_general(a, b, (dims, ((), ())), preferred_element_type=jnp.float32)

    expanded = [mm(normed[s], w_in[s], ((1,), (1,))).astype(jnp.bfloat16) for s in both]
    first_ext = extend(expanded, False)
    hidden_grad = [mm(ups[s], w_out[s], ((1,), (1,))) for s in both]
    fwd = (False, True)
    bwd = (True, False)
    first_conv = [
        apply_taps(first_ext[s], conv_taps[0], dilations[0], rows, fwd[s], margin).astype(jnp.bfloat16)
        for s in both
    ]
    second_ext = extend(first_conv, False)
    second_conv = [apply_taps(second_ext[s], conv_taps[1], dilations[1], rows, fwd[s], margin) for s in both]
    sig = [jax.nn.sigmoid(v) for v in second_conv]
    act = [second_conv[s] * sig[s] for s in both]
    exp_f = [e.astype(jnp.float32) for e in expanded]
    second_grad = [
        (hidden_grad[s] * exp_f[s] * sig[s] * (1.0 + second_conv[s] * (1.0 - sig[s]))).astype(jnp.bfloat16)
        for s in both
    ]
    grad_ext = extend(second_grad, True)
    gated = [(act[s] * exp_f[s]).astype(jnp.bfloat16) for s in both]
    block_out = jnp.concatenate(
        [
            (strands[s].astype(jnp.float32) + mm(gated[s], w_out[s], ((1,), (0,)))).astype(jnp.bfloat16)
            for s in both
        ],
        axis=1,
    )[None]
    grad_out = mm(gated[0], ups[0], ((0,), (0,))) + mm(gated[1], ups[1], ((0,), (0,)))[:, ::-1]
    grad_out = reduced(grad_out.astype(jnp.bfloat16))
    first_grad = [
        apply_taps(grad_ext[s], conv_taps[1], dilations[1], rows, bwd[s], margin).astype(jnp.bfloat16)
        for s in both
    ]
    inner_ext = extend(first_grad, True)
    tg1 = sum(taps_gradient(second_grad[s], second_ext[s], dilations[1], taps, fwd[s], margin) for s in both)
    tg0 = sum(taps_gradient(first_grad[s], first_ext[s], dilations[0], taps, fwd[s], margin) for s in both)
    carried = [apply_taps(inner_ext[s], conv_taps[0], dilations[0], rows, bwd[s], margin) for s in both]
    exp_grad = [(hidden_grad[s] * act[s] + carried[s]).astype(jnp.bfloat16) for s in both]
    grad_in = mm(exp_grad[0], normed[0], ((0,), (0,))) + mm(exp_grad[1], normed[1], ((0,), (0,)))[:, ::-1]
    taps_local = jnp.concatenate([tg0, tg1], axis=0)
    packed = jnp.concatenate([grad_in, jnp.pad(taps_local.T, ((0, 0), (0, 128 - 2 * taps)))], axis=1)
    packed = reduced(packed.astype(jnp.bfloat16))
    grad_in = packed[:, :half]
    tap_rows = lax.all_gather(packed[:, half : half + 128], "fsdp", axis=0, tiled=True)
    grad_taps = tap_rows[:, : 2 * taps].T.reshape(conv_taps.shape)
    f32 = jnp.float32
    return (block_out, grad_in.astype(f32), grad_out.astype(f32), grad_taps.astype(f32))


def reduced(terms):
    return lax.psum(lax.psum_scatter(terms, "fsdp", scatter_dimension=0, tiled=True), "ctx")


def solution(mesh):
    return jax.shard_map(
        body,
        mesh=mesh,
        in_specs=(
            P("fsdp", "ctx", None),
            P(),
            P("fsdp", None),
            P(),
            P(),
            P("fsdp", None),
            P("fsdp", "ctx", None),
        ),
        out_specs=(P("fsdp", "ctx", None), P("fsdp", None), P("fsdp", None), P()),
        check_vma=False,
    )
```

```python
import functools

import jax
import jax.numpy as jnp
from jax import lax
from jax.experimental import pallas as pl
from jax.experimental.pallas import tpu as pltpu
from jax.sharding import PartitionSpec as P

KERNEL = 7
MAXDIL = 64
MARGIN = (KERNEL - 1) * MAXDIL
BLOCK = 128
CHUNK = 128
norm_eps = 1e-05
F32 = jnp.float32
BF16 = jnp.bfloat16


def passed_along(value, axis, by):
    length = lax.axis_size(axis)
    pairs = [(i, i + by) for i in range(length) if 0 <= i + by < length]
    return lax.ppermute(value, axis, pairs)


def normalize(strand, norm_gain):
    floats = strand.astype(F32)
    inverse = lax.rsqrt(jnp.mean(floats * floats, axis=-1, keepdims=True) + norm_eps)
    return (floats * inverse * norm_gain).astype(BF16)


def mm(a, b, dims):
    return lax.dot_general(a, b, (dims, ((), ())), preferred_element_type=F32)


def starts(d, ahead):
    return [d * (KERNEL - 1 - t) if ahead else MARGIN - d * (KERNEL - 1 - t) for t in range(KERNEL)]


def join(ext, s, value, rim, ahead):
    rows = value.shape[0]
    if ahead:
        ext[s, 0:rows] = value.astype(F32)
        ext[s, rows : rows + MARGIN] = rim.astype(F32)
    else:
        ext[s, 0:MARGIN] = rim.astype(F32)
        ext[s, MARGIN : MARGIN + rows] = value.astype(F32)


def conv(ext, s, w_ref, f, first, offsets):
    acc = None
    for t in range(KERNEL):
        term = w_ref[f, t : t + 1, :] * ext[s, pl.ds(first + offsets[t], CHUNK), :]
        acc = term if acc is None else acc + term
    return acc


def tap_terms(sums, grad, ext, s, first, offsets):
    out = []
    for t in range(KERNEL):
        prod = grad * ext[s, pl.ds(first + offsets[t], CHUNK), :]
        part = prod[0:8]
        for k in range(1, CHUNK // 8):
            part = part + prod[8 * k : 8 * k + 8]
        out.append(sums[t] + part)
    return out


def no_sums():
    return [jnp.zeros((8, BLOCK), F32) for _ in range(KERNEL)]


def put_sums(out_ref, sums):
    for t in range(KERNEL):
        out_ref[t : t + 1, :] = jnp.sum(sums[t], axis=0, keepdims=True)


def first_kernel(d_ref, w_ref, n_ref, p_ref, e_ref, o_ref, ext):
    rows = o_ref.shape[1]
    for s in range(2):
        e = mm(n_ref[s], p_ref[...], ((1,), (1,))).astype(BF16)
        e_ref[s] = e
        ext[s] = e.astype(F32)
    for s in range(2):
        offsets = starts(d_ref[0], s == 1)

        @pl.loop(0, rows // CHUNK)
        def _(i):
            r = pl.multiple_of(i * CHUNK, CHUNK)
            o_ref[s, pl.ds(r, CHUNK), :] = conv(ext, s, w_ref, 0, r, offsets).astype(BF16)


def second_kernel(d_ref, w_ref, f_ref, rim_ref, e_ref, u_ref, p_ref, gated_ref, sg_ref, act_ref, tg_ref, ext, hg):
    rows = f_ref.shape[1]
    for s in range(2):
        join(ext, s, f_ref[s], rim_ref[s], s == 1)
        hg[s] = mm(u_ref[s], p_ref[...], ((1,), (1,)))
    sums = no_sums()
    for s in range(2):
        offsets = starts(d_ref[1], s == 1)
        own = 0 if s == 1 else MARGIN

        def step(i, sums):
            r = pl.multiple_of(i * CHUNK, CHUNK)
            here = pl.ds(r, CHUNK)
            v = conv(ext, s, w_ref, 1, r, offsets)
            sig = jax.nn.sigmoid(v)
            act = v * sig
            e = e_ref[s, pl.ds(pl.multiple_of(own + r, CHUNK), CHUNK), :].astype(F32)
            h = hg[s, here, :]
            gated_ref[s, here, :] = (act * e).astype(BF16)
            act_ref[s, here, :] = h * act
            grad = (h * e * sig * (1.0 + v * (1.0 - sig))).astype(BF16)
            sg_ref[s, here, :] = grad
            return tap_terms(sums, grad.astype(F32), ext, s, r, offsets)

        sums = lax.fori_loop(0, rows // CHUNK, step, sums)
    put_sums(tg_ref, sums)


def third_kernel(d_ref, w_ref, sg_ref, rim_ref, e_ref, fg_ref, tg_ref, ext, eext):
    rows = sg_ref.shape[1]
    for s in range(2):
        join(ext, s, sg_ref[s], rim_ref[s], s == 0)
        eext[s] = e_ref[s].astype(F32)
    sums = no_sums()
    for s in range(2):
        offsets = starts(d_ref[1], s == 0)
        behind = starts(d_ref[0], s == 1)

        def step(i, sums):
            r = pl.multiple_of(i * CHUNK, CHUNK)
            grad = conv(ext, s, w_ref, 1, r, offsets).astype(BF16)
            fg_ref[s, pl.ds(r, CHUNK), :] = grad
            return tap_terms(sums, grad.astype(F32), eext, s, r, behind)

        sums = lax.fori_loop(0, rows // CHUNK, step, sums)
    put_sums(tg_ref, sums)


def fourth_kernel(d_ref, w_ref, fg_ref, rim_ref, act_ref, eg_ref, ext):
    rows = fg_ref.shape[1]
    for s in range(2):
        join(ext, s, fg_ref[s], rim_ref[s], s == 0)
    for s in range(2):
        offsets = starts(d_ref[0], s == 0)

        @pl.loop(0, rows // CHUNK)
        def _(i):
            r = pl.multiple_of(i * CHUNK, CHUNK)
            here = pl.ds(r, CHUNK)
            eg_ref[s, here, :] = (act_ref[s, here, :] + conv(ext, s, w_ref, 0, r, offsets)).astype(BF16)


def hidden_block(rows):
    return pl.BlockSpec((2, rows, BLOCK), lambda j: (0, 0, j))


def call(kernel, inner, in_specs, outs, scratch, args, ops):
    specs = [pl.BlockSpec(memory_space=pltpu.SMEM), pl.BlockSpec((2, KERNEL, BLOCK), lambda j: (0, 0, j))]
    return pl.pallas_call(
        kernel,
        grid=(inner // BLOCK,),
        in_specs=specs + in_specs,
        out_specs=[o[1] for o in outs],
        out_shape=[o[0] for o in outs],
        scratch_shapes=[pltpu.VMEM(s, F32) for s in scratch],
        compiler_params=pltpu.CompilerParams(vmem_limit_bytes=32 << 20),
        cost_estimate=pl.CostEstimate(flops=ops, bytes_accessed=8 << 20, transcendentals=0),
    )(*args)


def rims(values, backward):
    got = []
    for s in range(2):
        if (s == 1) != backward:
            got.append(passed_along(values[s][:MARGIN], "ctx", -1))
        else:
            got.append(passed_along(values[s][-MARGIN:], "ctx", 1))
    return got


def body(states, norm_gain, in_proj, conv_taps, dilations, out_proj, cotangent):
    half = states.shape[2] // 2
    rows = states.shape[1]
    inner = conv_taps.shape[2]
    full_in, full_out = weights(in_proj, out_proj)
    flip = jnp.eye(half, dtype=BF16)[::-1]

    def flipped(a):
        return mm(a, flip, ((1,), (0,))).astype(BF16)

    strand = [states[0, :, :half], flipped(states[0, :, half:])]
    ups = jnp.stack([cotangent[0, :, :half], flipped(cotangent[0, :, half:])])
    rim = rims(strand, False)
    ext = jnp.stack([jnp.concatenate([rim[0], strand[0]]), jnp.concatenate([strand[1], rim[1]])])
    normed_ext = normalize(ext, norm_gain)

    wide = rows + MARGIN
    proj = pl.BlockSpec((BLOCK, half), lambda j: (j, 0))
    whole_rows = pl.BlockSpec((2, rows, half), lambda j: (0, 0, 0))

    def out(n, dtype=BF16):
        return (jax.ShapeDtypeStruct((2, n, inner), dtype), hidden_block(n))

    tap_out = (jax.ShapeDtypeStruct((KERNEL, inner), F32), pl.BlockSpec((KERNEL, BLOCK), lambda j: (0, j)))
    scr = (2, wide, BLOCK)
    expanded, first = call(
        first_kernel, inner,
        [pl.BlockSpec((2, wide, half), lambda j: (0, 0, 0)), proj],
        [out(wide), out(rows)], [scr],
        (dilations, conv_taps, normed_ext, full_in), 2 * 10**9,
    )
    first_rim = jnp.stack(rims(first, False))
    gated, second_grad, act_term, tg1 = call(
        second_kernel, inner,
        [hidden_block(rows), hidden_block(MARGIN), hidden_block(wide), whole_rows, proj],
        [out(rows), out(rows), out(rows, F32), tap_out], [scr, (2, rows, BLOCK)],
        (dilations, conv_taps, first, first_rim, expanded, ups, full_out), 2 * 10**9,
    )
    second_rim = jnp.stack(rims(second_grad, True))
    flat_gated = gated.reshape(2 * rows, inner)
    grad_out = mm(flat_gated, ups.reshape(2 * rows, half), ((0,), (0,)))
    first_grad, tg0 = call(
        third_kernel, inner,
        [hidden_block(rows), hidden_block(MARGIN), hidden_block(wide)],
        [out(rows), tap_out], [scr, scr],
        (dilations, conv_taps, second_grad, second_rim, expanded), 10**9,
    )
    third_rim = jnp.stack(rims(first_grad, True))
    mixed = mm(flat_gated, full_out, ((1,), (0,))).reshape(2, rows, half)
    made = [(strand[s].astype(F32) + mixed[s]).astype(BF16) for s in range(2)]
    block_out = jnp.concatenate([made[0], flipped(made[1])], axis=1)[None]
    (exp_grad,) = call(
        fourth_kernel, inner,
        [hidden_block(rows), hidden_block(MARGIN), hidden_block(rows)],
        [out(rows)], [scr],
        (dilations, conv_taps, first_grad, third_rim, act_term), 10**9,
    )
    grad_in = sum(mm(exp_grad[s], normalize(strand[s], norm_gain), ((0,), (0,))) for s in range(2))
    return (block_out, *summed(grad_in, grad_out, jnp.stack([tg0, tg1])))


def weights(in_proj, out_proj):
    half = in_proj.shape[1]
    both = lax.all_gather(jnp.concatenate([in_proj, out_proj], axis=1), "fsdp", axis=0, tiled=True)
    return both[:, :half], both[:, half:]


def summed(grad_in, grad_out, taps):
    half = grad_in.shape[1]
    count = taps.shape[0] * taps.shape[1]
    cols = taps.reshape(count, taps.shape[2]).T
    packed = jnp.concatenate([grad_in, grad_out, jnp.pad(cols, ((0, 0), (0, 128 - count)))], axis=1).astype(BF16)
    packed = lax.psum(lax.psum_scatter(packed, "fsdp", scatter_dimension=0, tiled=True), "ctx")
    tap_rows = lax.all_gather(packed[:, 2 * half :], "fsdp", axis=0, tiled=True)
    grad_taps = tap_rows[:, :count].T.reshape(taps.shape)
    return packed[:, :half].astype(F32), packed[:, half : 2 * half].astype(F32), grad_taps.astype(F32)


def solution(mesh):
    return jax.shard_map(
        body,
        mesh=mesh,
        in_specs=(
            P("fsdp", "ctx", None),
            P(),
            P("fsdp", None),
            P(),
            P(),
            P("fsdp", None),
            P("fsdp", "ctx", None),
        ),
        out_specs=(P("fsdp", "ctx", None), P("fsdp", None), P("fsdp", None), P()),
        check_vma=False,
    )
```

```python
import functools

import jax
import jax.numpy as jnp
from jax import lax
from jax.experimental import pallas as pl
from jax.experimental.pallas import tpu as pltpu
from jax.sharding import PartitionSpec as P

KERNEL = 7
MAXDIL = 64
MARGIN = (KERNEL - 1) * MAXDIL
BLOCK = 128
CHUNK = 128
norm_eps = 1e-05
F32 = jnp.float32
BF16 = jnp.bfloat16


def passed_along(value, axis, by):
    length = lax.axis_size(axis)
    pairs = [(i, i + by) for i in range(length) if 0 <= i + by < length]
    return lax.ppermute(value, axis, pairs)


def normalize(strand, norm_gain):
    floats = strand.astype(F32)
    inverse = lax.rsqrt(jnp.mean(floats * floats, axis=-1, keepdims=True) + norm_eps)
    return (floats * inverse * norm_gain).astype(BF16)


def mm(a, b, dims):
    return lax.dot_general(a, b, (dims, ((), ())), preferred_element_type=F32)


def starts(d, ahead):
    return [d * (KERNEL - 1 - t) if ahead else MARGIN - d * (KERNEL - 1 - t) for t in range(KERNEL)]


def join(ext, s, value, rim, ahead):
    rows = value.shape[0]
    if ahead:
        ext[s, 0:rows] = value.astype(F32)
        ext[s, rows : rows + MARGIN] = rim.astype(F32)
    else:
        ext[s, 0:MARGIN] = rim.astype(F32)
        ext[s, MARGIN : MARGIN + rows] = value.astype(F32)


def conv(ext, s, w_ref, f, first, offsets):
    acc = None
    for t in range(KERNEL):
        term = w_ref[f, t : t + 1, :] * ext[s, pl.ds(first + offsets[t], CHUNK), :]
        acc = term if acc is None else acc + term
    return acc


def tap_terms(sums, grad, ext, s, first, offsets):
    out = []
    for t in range(KERNEL):
        prod = grad * ext[s, pl.ds(first + offsets[t], CHUNK), :]
        part = prod[0:8]
        for k in range(1, CHUNK // 8):
            part = part + prod[8 * k : 8 * k + 8]
        out.append(sums[t] + part)
    return out


def no_sums():
    return [jnp.zeros((8, BLOCK), F32) for _ in range(KERNEL)]


def put_sums(out_ref, sums):
    for t in range(KERNEL):
        out_ref[t : t + 1, :] = jnp.sum(sums[t], axis=0, keepdims=True)


def first_kernel(d_ref, w_ref, n_ref, p_ref, e_ref, o_ref, ext):
    rows = o_ref.shape[1]
    for s in range(2):
        e = mm(n_ref[s], p_ref[...], ((1,), (1,))).astype(BF16)
        e_ref[s] = e
        ext[s] = e.astype(F32)
    for s in range(2):
        offsets = starts(d_ref[0], s == 1)

        @pl.loop(0, rows // CHUNK)
        def _(i):
            r = pl.multiple_of(i * CHUNK, CHUNK)
            o_ref[s, pl.ds(r, CHUNK), :] = conv(ext, s, w_ref, 0, r, offsets).astype(BF16)


def second_kernel(d_ref, w_ref, f_ref, rim_ref, e_ref, u_ref, p_ref, gated_ref, sg_ref, act_ref, tg_ref, ext, hg):
    rows = f_ref.shape[1]
    for s in range(2):
        join(ext, s, f_ref[s], rim_ref[s], s == 1)
        hg[s] = mm(u_ref[s], p_ref[...], ((1,), (1,)))
    sums = no_sums()
    for s in range(2):
        offsets = starts(d_ref[1], s == 1)
        own = 0 if s == 1 else MARGIN

        def step(i, sums):
            r = pl.multiple_of(i * CHUNK, CHUNK)
            here = pl.ds(r, CHUNK)
            v = conv(ext, s, w_ref, 1, r, offsets)
            sig = jax.nn.sigmoid(v)
            act = v * sig
            e = e_ref[s, pl.ds(pl.multiple_of(own + r, CHUNK), CHUNK), :].astype(F32)
            h = hg[s, here, :]
            gated_ref[s, here, :] = (act * e).astype(BF16)
            act_ref[s, here, :] = h * act
            grad = (h * e * sig * (1.0 + v * (1.0 - sig))).astype(BF16)
            sg_ref[s, here, :] = grad
            return tap_terms(sums, grad.astype(F32), ext, s, r, offsets)

        sums = lax.fori_loop(0, rows // CHUNK, step, sums)
    put_sums(tg_ref, sums)


def third_kernel(d_ref, w_ref, sg_ref, rim_ref, e_ref, fg_ref, tg_ref, ext, eext):
    rows = sg_ref.shape[1]
    for s in range(2):
        join(ext, s, sg_ref[s], rim_ref[s], s == 0)
        eext[s] = e_ref[s].astype(F32)
    sums = no_sums()
    for s in range(2):
        offsets = starts(d_ref[1], s == 0)
        behind = starts(d_ref[0], s == 1)

        def step(i, sums):
            r = pl.multiple_of(i * CHUNK, CHUNK)
            grad = conv(ext, s, w_ref, 1, r, offsets).astype(BF16)
            fg_ref[s, pl.ds(r, CHUNK), :] = grad
            return tap_terms(sums, grad.astype(F32), eext, s, r, behind)

        sums = lax.fori_loop(0, rows // CHUNK, step, sums)
    put_sums(tg_ref, sums)


def fourth_kernel(d_ref, w_ref, fg_ref, rim_ref, act_ref, eg_ref, ext):
    rows = fg_ref.shape[1]
    for s in range(2):
        join(ext, s, fg_ref[s], rim_ref[s], s == 0)
    for s in range(2):
        offsets = starts(d_ref[0], s == 0)

        @pl.loop(0, rows // CHUNK)
        def _(i):
            r = pl.multiple_of(i * CHUNK, CHUNK)
            here = pl.ds(r, CHUNK)
            eg_ref[s, here, :] = (act_ref[s, here, :] + conv(ext, s, w_ref, 0, r, offsets)).astype(BF16)


def hidden_block(rows):
    return pl.BlockSpec((2, rows, BLOCK), lambda j: (0, 0, j))


def call(kernel, inner, in_specs, outs, scratch, args, ops):
    specs = [pl.BlockSpec(memory_space=pltpu.SMEM), pl.BlockSpec((2, KERNEL, BLOCK), lambda j: (0, 0, j))]
    return pl.pallas_call(
        kernel,
        grid=(inner // BLOCK,),
        in_specs=specs + in_specs,
        out_specs=[o[1] for o in outs],
        out_shape=[o[0] for o in outs],
        scratch_shapes=[pltpu.VMEM(s, F32) for s in scratch],
        compiler_params=pltpu.CompilerParams(vmem_limit_bytes=32 << 20),
        cost_estimate=pl.CostEstimate(flops=ops, bytes_accessed=8 << 20, transcendentals=0),
    )(*args)


def rims(values, backward):
    got = []
    for s in range(2):
        if (s == 1) != backward:
            got.append(passed_along(values[s][:MARGIN], "ctx", -1))
        else:
            got.append(passed_along(values[s][-MARGIN:], "ctx", 1))
    return got


def body(states, norm_gain, in_proj, conv_taps, dilations, out_proj, cotangent):
    half = states.shape[2] // 2
    rows = states.shape[1]
    inner = conv_taps.shape[2]
    full_in, full_out = weights(in_proj, out_proj)
    flip = jnp.eye(half, dtype=BF16)[::-1]

    def flipped(a):
        return mm(a, flip, ((1,), (0,))).astype(BF16)

    strand = [states[0, :, :half], flipped(states[0, :, half:])]
    ups = jnp.stack([cotangent[0, :, :half], flipped(cotangent[0, :, half:])])
    rim = rims(strand, False)
    ext = jnp.stack([jnp.concatenate([rim[0], strand[0]]), jnp.concatenate([strand[1], rim[1]])])
    normed_ext = normalize(ext, norm_gain)

    wide = rows + MARGIN
    proj = pl.BlockSpec((BLOCK, half), lambda j: (j, 0))
    whole_rows = pl.BlockSpec((2, rows, half), lambda j: (0, 0, 0))

    def out(n, dtype=BF16):
        return (jax.ShapeDtypeStruct((2, n, inner), dtype), hidden_block(n))

    tap_out = (jax.ShapeDtypeStruct((KERNEL, inner), F32), pl.BlockSpec((KERNEL, BLOCK), lambda j: (0, j)))
    scr = (2, wide, BLOCK)
    expanded, first = call(
        first_kernel, inner,
        [pl.BlockSpec((2, wide, half), lambda j: (0, 0, 0)), proj],
        [out(wide), out(rows)], [scr],
        (dilations, conv_taps, normed_ext, full_in), 2 * 10**9,
    )
    first_rim = jnp.stack(rims(first, False))
    gated, second_grad, act_term, tg1 = call(
        second_kernel, inner,
        [hidden_block(rows), hidden_block(MARGIN), hidden_block(wide), whole_rows, proj],
        [out(rows), out(rows), out(rows, F32), tap_out], [scr, (2, rows, BLOCK)],
        (dilations, conv_taps, first, first_rim, expanded, ups, full_out), 2 * 10**9,
    )
    second_rim = jnp.stack(rims(second_grad, True))
    flat_gated = gated.reshape(2 * rows, inner)
    grad_out = mm(flat_gated, ups.reshape(2 * rows, half), ((0,), (0,)))
    first_grad, tg0 = call(
        third_kernel, inner,
        [hidden_block(rows), hidden_block(MARGIN), hidden_block(wide)],
        [out(rows), tap_out], [scr, scr],
        (dilations, conv_taps, second_grad, second_rim, expanded), 10**9,
    )
    third_rim = jnp.stack(rims(first_grad, True))
    mixed = mm(flat_gated, full_out, ((1,), (0,))).reshape(2, rows, half)
    made = [(strand[s].astype(F32) + mixed[s]).astype(BF16) for s in range(2)]
    block_out = jnp.concatenate([made[0], flipped(made[1])], axis=1)[None]
    (exp_grad,) = call(
        fourth_kernel, inner,
        [hidden_block(rows), hidden_block(MARGIN), hidden_block(rows)],
        [out(rows)], [scr],
        (dilations, conv_taps, first_grad, third_rim, act_term), 10**9,
    )
    grad_in = sum(mm(exp_grad[s], normalize(strand[s], norm_gain), ((0,), (0,))) for s in range(2))
    return (block_out, *summed(grad_in, grad_out, jnp.stack([tg0, tg1])))


def gathered(x, axis):
    n = lax.axis_size(axis)
    me = lax.axis_index(axis)
    parts = lax.dynamic_update_slice_in_dim(jnp.zeros((n, *x.shape), x.dtype), x[None], me, 0)
    for k in range(1, n):
        got = lax.ppermute(x, axis, [(i, (i + k) % n) for i in range(n)])
        parts = lax.dynamic_update_slice_in_dim(parts, got[None], (me - k + n) % n, 0)
    return parts.reshape(n * x.shape[0], *x.shape[1:])


def swapped(x, bit):
    return lax.ppermute(x, "ctx", [(i, i ^ (1 << bit)) for i in range(lax.axis_size("ctx"))])


def weights(in_proj, out_proj):
    even = lax.axis_index("ctx") % 2 == 0
    mine = gathered(jnp.where(even, in_proj, out_proj), "fsdp")
    other = swapped(mine, 0)
    return jnp.where(even, mine, other), jnp.where(even, other, mine)


def summed(grad_in, grad_out, taps):
    half = grad_in.shape[1]
    count = taps.shape[0] * taps.shape[1]
    owners = lax.axis_size("fsdp")
    per = grad_in.shape[0] // owners
    me = lax.axis_index("ctx")
    zone = lax.axis_index("fsdp")
    bits = lax.axis_size("ctx").bit_length() - 1
    cols = taps.reshape(count, taps.shape[2]).T
    packed = jnp.concatenate([grad_in, grad_out, jnp.pad(cols, ((0, 0), (0, 128 - count)))], axis=1)
    groups = packed.shape[1] // 128
    x = packed.reshape(owners, per, groups, 128).transpose(0, 2, 1, 3).reshape(owners, groups * per, 128)
    for bit in range(bits):
        upper = (me >> bit) % 2 == 1
        middle = x.shape[1] // 2
        low, high = x[:, :middle], x[:, middle:]
        got = swapped(jnp.where(upper, low, high).astype(BF16), bit)
        x = jnp.where(upper, high, low) + got.astype(F32)
    total = lax.dynamic_index_in_dim(x, zone, 0, False)
    sent = x.astype(BF16)
    for k in range(1, owners):
        piece = lax.dynamic_index_in_dim(sent, (zone + k) % owners, 0, False)
        got = lax.ppermute(piece, "fsdp", [(i, (i + k) % owners) for i in range(owners)])
        total = total + got.astype(F32)
    x = total.astype(BF16)
    for bit in reversed(range(bits)):
        upper = (me >> bit) % 2 == 1
        got = swapped(x, bit)
        x = jnp.concatenate([jnp.where(upper, got, x), jnp.where(upper, x, got)], axis=0)
    x = x.reshape(groups, per, 128)
    wide = x[:-1].transpose(1, 0, 2).reshape(per, 2 * half)
    tap_rows = gathered(x[-1], "fsdp")
    grad_taps = tap_rows[:, :count].T.reshape(taps.shape)
    return wide[:, :half].astype(F32), wide[:, half:].astype(F32), grad_taps.astype(F32)


def solution(mesh):
    return jax.shard_map(
        body,
        mesh=mesh,
        in_specs=(
            P("fsdp", "ctx", None),
            P(),
            P("fsdp", None),
            P(),
            P(),
            P("fsdp", None),
            P("fsdp", "ctx", None),
        ),
        out_specs=(P("fsdp", "ctx", None), P("fsdp", None), P("fsdp", None), P()),
        check_vma=False,
    )
```

```python
import functools

import jax
import jax.numpy as jnp
from jax import lax
from jax.experimental import pallas as pl
from jax.experimental.pallas import tpu as pltpu
from jax.sharding import PartitionSpec as P

KERNEL = 7
MAXDIL = 64
MARGIN = (KERNEL - 1) * MAXDIL
BLOCK = 128
CHUNK = 128
norm_eps = 1e-05
F32 = jnp.float32
BF16 = jnp.bfloat16


def passed_along(value, axis, by):
    length = lax.axis_size(axis)
    pairs = [(i, i + by) for i in range(length) if 0 <= i + by < length]
    return lax.ppermute(value, axis, pairs)


def normalize(strand, norm_gain):
    floats = strand.astype(F32)
    inverse = lax.rsqrt(jnp.mean(floats * floats, axis=-1, keepdims=True) + norm_eps)
    return (floats * inverse * norm_gain).astype(BF16)


def mm(a, b, dims):
    return lax.dot_general(a, b, (dims, ((), ())), preferred_element_type=F32)


def starts(d, ahead):
    return [d * (KERNEL - 1 - t) if ahead else MARGIN - d * (KERNEL - 1 - t) for t in range(KERNEL)]


def join(ext, s, value, rim, ahead):
    rows = value.shape[0]
    if ahead:
        ext[s, 0:rows] = value.astype(F32)
        ext[s, rows : rows + MARGIN] = rim.astype(F32)
    else:
        ext[s, 0:MARGIN] = rim.astype(F32)
        ext[s, MARGIN : MARGIN + rows] = value.astype(F32)


def conv(ext, s, w_ref, f, first, offsets):
    acc = None
    for t in range(KERNEL):
        term = w_ref[f, t : t + 1, :] * ext[s, pl.ds(first + offsets[t], CHUNK), :]
        acc = term if acc is None else acc + term
    return acc


def tap_terms(sums, grad, ext, s, first, offsets):
    out = []
    for t in range(KERNEL):
        prod = grad * ext[s, pl.ds(first + offsets[t], CHUNK), :]
        part = prod[0:8]
        for k in range(1, CHUNK // 8):
            part = part + prod[8 * k : 8 * k + 8]
        out.append(sums[t] + part)
    return out


def no_sums():
    return [jnp.zeros((8, BLOCK), F32) for _ in range(KERNEL)]


def put_sums(out_ref, sums):
    for t in range(KERNEL):
        out_ref[t : t + 1, :] = jnp.sum(sums[t], axis=0, keepdims=True)


def first_kernel(d_ref, w_ref, n_ref, p_ref, e_ref, o_ref, ext):
    rows = o_ref.shape[1]
    for s in range(2):
        e = mm(n_ref[s], p_ref[...], ((1,), (1,))).astype(BF16)
        e_ref[s] = e
        ext[s] = e.astype(F32)
    for s in range(2):
        offsets = starts(d_ref[0], s == 1)

        @pl.loop(0, rows // CHUNK)
        def _(i):
            r = pl.multiple_of(i * CHUNK, CHUNK)
            o_ref[s, pl.ds(r, CHUNK), :] = conv(ext, s, w_ref, 0, r, offsets).astype(BF16)


def second_kernel(d_ref, w_ref, f_ref, rim_ref, e_ref, u_ref, p_ref, gated_ref, sg_ref, act_ref, tg_ref, ext, hg):
    rows = f_ref.shape[1]
    for s in range(2):
        join(ext, s, f_ref[s], rim_ref[s], s == 1)
        hg[s] = mm(u_ref[s], p_ref[...], ((1,), (1,)))
    sums = no_sums()
    for s in range(2):
        offsets = starts(d_ref[1], s == 1)
        own = 0 if s == 1 else MARGIN

        def step(i, sums):
            r = pl.multiple_of(i * CHUNK, CHUNK)
            here = pl.ds(r, CHUNK)
            v = conv(ext, s, w_ref, 1, r, offsets)
            sig = jax.nn.sigmoid(v)
            act = v * sig
            e = e_ref[s, pl.ds(pl.multiple_of(own + r, CHUNK), CHUNK), :].astype(F32)
            h = hg[s, here, :]
            gated_ref[s, here, :] = (act * e).astype(BF16)
            act_ref[s, here, :] = h * act
            grad = (h * e * sig * (1.0 + v * (1.0 - sig))).astype(BF16)
            sg_ref[s, here, :] = grad
            return tap_terms(sums, grad.astype(F32), ext, s, r, offsets)

        sums = lax.fori_loop(0, rows // CHUNK, step, sums)
    put_sums(tg_ref, sums)


def third_kernel(d_ref, w_ref, sg_ref, rim_ref, e_ref, fg_ref, tg_ref, ext, eext):
    rows = sg_ref.shape[1]
    for s in range(2):
        join(ext, s, sg_ref[s], rim_ref[s], s == 0)
        eext[s] = e_ref[s].astype(F32)
    sums = no_sums()
    for s in range(2):
        offsets = starts(d_ref[1], s == 0)
        behind = starts(d_ref[0], s == 1)

        def step(i, sums):
            r = pl.multiple_of(i * CHUNK, CHUNK)
            grad = conv(ext, s, w_ref, 1, r, offsets).astype(BF16)
            fg_ref[s, pl.ds(r, CHUNK), :] = grad
            return tap_terms(sums, grad.astype(F32), eext, s, r, behind)

        sums = lax.fori_loop(0, rows // CHUNK, step, sums)
    put_sums(tg_ref, sums)


def fourth_kernel(d_ref, w_ref, fg_ref, rim_ref, act_ref, eg_ref, ext):
    rows = fg_ref.shape[1]
    for s in range(2):
        join(ext, s, fg_ref[s], rim_ref[s], s == 0)
    for s in range(2):
        offsets = starts(d_ref[0], s == 0)

        @pl.loop(0, rows // CHUNK)
        def _(i):
            r = pl.multiple_of(i * CHUNK, CHUNK)
            here = pl.ds(r, CHUNK)
            eg_ref[s, here, :] = (act_ref[s, here, :] + conv(ext, s, w_ref, 0, r, offsets)).astype(BF16)


def hidden_block(rows):
    return pl.BlockSpec((2, rows, BLOCK), lambda j: (0, 0, j))


def call(kernel, inner, in_specs, outs, scratch, args, ops):
    specs = [pl.BlockSpec(memory_space=pltpu.SMEM), pl.BlockSpec((2, KERNEL, BLOCK), lambda j: (0, 0, j))]
    return pl.pallas_call(
        kernel,
        grid=(inner // BLOCK,),
        in_specs=specs + in_specs,
        out_specs=[o[1] for o in outs],
        out_shape=[o[0] for o in outs],
        scratch_shapes=[pltpu.VMEM(s, F32) for s in scratch],
        compiler_params=pltpu.CompilerParams(vmem_limit_bytes=32 << 20),
        cost_estimate=pl.CostEstimate(flops=ops, bytes_accessed=8 << 20, transcendentals=0),
    )(*args)


def rims(values, backward):
    got = []
    for s in range(2):
        if (s == 1) != backward:
            got.append(passed_along(values[s][:MARGIN], "ctx", -1))
        else:
            got.append(passed_along(values[s][-MARGIN:], "ctx", 1))
    return got


def body(states, norm_gain, in_proj, conv_taps, dilations, out_proj, cotangent):
    half = states.shape[2] // 2
    rows = states.shape[1]
    inner = conv_taps.shape[2]
    full_in, full_out = weights(in_proj, out_proj)
    flip = jnp.eye(half, dtype=BF16)[::-1]

    def flipped(a):
        return mm(a, flip, ((1,), (0,))).astype(BF16)

    strand = [states[0, :, :half], flipped(states[0, :, half:])]
    ups = jnp.stack([cotangent[0, :, :half], flipped(cotangent[0, :, half:])])
    rim = rims(strand, False)
    ext = jnp.stack([jnp.concatenate([rim[0], strand[0]]), jnp.concatenate([strand[1], rim[1]])])
    normed_ext = normalize(ext, norm_gain)

    wide = rows + MARGIN
    proj = pl.BlockSpec((BLOCK, half), lambda j: (j, 0))
    whole_rows = pl.BlockSpec((2, rows, half), lambda j: (0, 0, 0))

    def out(n, dtype=BF16):
        return (jax.ShapeDtypeStruct((2, n, inner), dtype), hidden_block(n))

    tap_out = (jax.ShapeDtypeStruct((KERNEL, inner), F32), pl.BlockSpec((KERNEL, BLOCK), lambda j: (0, j)))
    scr = (2, wide, BLOCK)
    expanded, first = call(
        first_kernel, inner,
        [pl.BlockSpec((2, wide, half), lambda j: (0, 0, 0)), proj],
        [out(wide), out(rows)], [scr],
        (dilations, conv_taps, normed_ext, full_in), 2 * 10**9,
    )
    first_rim = jnp.stack(rims(first, False))
    gated, second_grad, act_term, tg1 = call(
        second_kernel, inner,
        [hidden_block(rows), hidden_block(MARGIN), hidden_block(wide), whole_rows, proj],
        [out(rows), out(rows), out(rows, F32), tap_out], [scr, (2, rows, BLOCK)],
        (dilations, conv_taps, first, first_rim, expanded, ups, full_out), 2 * 10**9,
    )
    second_rim = jnp.stack(rims(second_grad, True))
    flat_gated = gated.reshape(2 * rows, inner)
    grad_out = mm(flat_gated, ups.reshape(2 * rows, half), ((0,), (0,)))
    first_grad, tg0 = call(
        third_kernel, inner,
        [hidden_block(rows), hidden_block(MARGIN), hidden_block(wide)],
        [out(rows), tap_out], [scr, scr],
        (dilations, conv_taps, second_grad, second_rim, expanded), 10**9,
    )
    third_rim = jnp.stack(rims(first_grad, True))
    mixed = mm(flat_gated, full_out, ((1,), (0,))).reshape(2, rows, half)
    made = [(strand[s].astype(F32) + mixed[s]).astype(BF16) for s in range(2)]
    block_out = jnp.concatenate([made[0], flipped(made[1])], axis=1)[None]
    (exp_grad,) = call(
        fourth_kernel, inner,
        [hidden_block(rows), hidden_block(MARGIN), hidden_block(rows)],
        [out(rows)], [scr],
        (dilations, conv_taps, first_grad, third_rim, act_term), 10**9,
    )
    grad_in = sum(mm(exp_grad[s], normalize(strand[s], norm_gain), ((0,), (0,))) for s in range(2))
    return (block_out, *summed(grad_in, grad_out, jnp.stack([tg0, tg1])))


def gathered(x, axis):
    n = lax.axis_size(axis)
    me = lax.axis_index(axis)
    parts = lax.dynamic_update_slice_in_dim(jnp.zeros((n, *x.shape), x.dtype), x[None], me, 0)
    for k in range(1, n):
        got = lax.ppermute(x, axis, [(i, (i + k) % n) for i in range(n)])
        parts = lax.dynamic_update_slice_in_dim(parts, got[None], (me - k + n) % n, 0)
    return parts.reshape(n * x.shape[0], *x.shape[1:])


def swapped(x, bit):
    return lax.ppermute(x, "ctx", [(i, i ^ (1 << bit)) for i in range(lax.axis_size("ctx"))])


def weights(in_proj, out_proj):
    even = lax.axis_index("ctx") % 2 == 0
    mine = gathered(jnp.where(even, in_proj, out_proj), "fsdp")
    other = swapped(mine, 0)
    return jnp.where(even, mine, other), jnp.where(even, other, mine)


def summed(grad_in, grad_out, taps):
    half = grad_in.shape[1]
    count = taps.shape[0] * taps.shape[1]
    owners = lax.axis_size("fsdp")
    per = grad_in.shape[0] // owners
    me = lax.axis_index("ctx")
    zone = lax.axis_index("fsdp")
    bits = lax.axis_size("ctx").bit_length() - 1
    cols = taps.reshape(count, taps.shape[2]).T
    packed = jnp.concatenate([grad_in, grad_out, jnp.pad(cols, ((0, 0), (0, 128 - count)))], axis=1)
    x = packed.reshape(owners, per, packed.shape[1])
    for bit in range(bits):
        upper = (me >> bit) % 2 == 1
        middle = x.shape[1] // 2
        low, high = x[:, :middle], x[:, middle:]
        got = swapped(jnp.where(upper, low, high).astype(BF16), bit)
        x = jnp.where(upper, high, low) + got.astype(F32)
    total = lax.dynamic_index_in_dim(x, zone, 0, False)
    sent = x.astype(BF16)
    for k in range(1, owners):
        piece = lax.dynamic_index_in_dim(sent, (zone + k) % owners, 0, False)
        got = lax.ppermute(piece, "fsdp", [(i, (i + k) % owners) for i in range(owners)])
        total = total + got.astype(F32)
    x = total.astype(BF16)
    for bit in reversed(range(bits)):
        upper = (me >> bit) % 2 == 1
        got = swapped(x, bit)
        x = jnp.concatenate([jnp.where(upper, got, x), jnp.where(upper, x, got)], axis=0)
    tap_rows = gathered(x[:, 2 * half :], "fsdp")
    grad_taps = tap_rows[:, :count].T.reshape(taps.shape)
    return x[:, :half].astype(F32), x[:, half : 2 * half].astype(F32), grad_taps.astype(F32)


def solution(mesh):
    return jax.shard_map(
        body,
        mesh=mesh,
        in_specs=(
            P("fsdp", "ctx", None),
            P(),
            P("fsdp", None),
            P(),
            P(),
            P("fsdp", None),
            P("fsdp", "ctx", None),
        ),
        out_specs=(P("fsdp", "ctx", None), P("fsdp", None), P("fsdp", None), P()),
        check_vma=False,
    )
```
